512 devices in a mesh: row: 128 (over y, x_hi, z), rep: 4 (over x_lo, core).
Axes of the slice: x: 4 (x_hi: 2, x_lo: 2; x = x_hi * 2 + x_lo), y: 8, z: 8, core: 2. Of those that a mesh axis runs over, the one named last changes fastest.
Arguments:
- features_t: bfloat16 [128, 32768], P('rep', 'row'), may hold values from -6 to 6
- tile_values: bfloat16 [16384, 128, 128], P('row'), may hold values from -0.09375 to 0.09375
- tile_rows: int32 [16384], P('row'), may hold values from 0 to 1, as said below
- tile_cols: int32 [16384], P('row'), may hold values from 0 to 255, as said below
- tile_count: int32 [128], P('row'), may hold values from 1 to 128, as said below
- weight: bfloat16 [128, 256], replicated, may hold values from -0.5 to 0.5
- cotangent: bfloat16 [32768, 256], P('row', 'rep'), may hold values from -0.078125 to 0.078125
Outputs:
- hidden: bfloat16 [32768, 256], P('row', 'rep')
- d_weight: float32 [128, 256], P('rep')
The draws below stay inside these ranges and needn't reach their ends.
Inputs may be any that keep to these rules, and one draw needn't show every extreme that they name: `tile_rows`: within one node block all 128 slots name distinct (tile row, tile column) pairs; slots at or past the block's count are padding and carry no adjacency. `tile_cols`: tile column of each slot, distinct pairs with tile_rows within a block. Live slots of a block are its first tile_count slots; some block is full.
All inputs are finite; a program needn't handle non-finite values.
Results may differ from the reference program's by a relative error of at most 0.0054.
Values may be sent and summed in bfloat16 or wider, within the bound.
A program may use at most 64 MiB of HBM per device.

```python
import jax
import jax.numpy as jnp
from jax import lax

F = 128
HID = 256
TILE = 128
TROWS = 2
LT = 128
NTILES = 256
NODES = 32768
N_ROW = 128


def tile_codes(key):
    blocks = NTILES // TROWS
    block_keys = jax.random.split(key, blocks)
    codes = jax.vmap(lambda k: jax.random.permutation(k, TROWS * NTILES)[:LT])(block_keys)
    return codes.reshape(blocks * LT).astype(jnp.int32)


def draw_tile_rows(key, part):
    codes = tile_codes(key)
    return (codes // NTILES).astype(jnp.int32)


def draw_tile_cols(key, part):
    codes = tile_codes(key)
    return (codes % NTILES).astype(jnp.int32)


def draw_tile_count(key, part):
    key = jax.random.fold_in(key, 7)
    blocks = NTILES // TROWS
    first_key, second_key, third_key = jax.random.split(key, 3)
    first = jax.random.randint(first_key, (blocks,), 0, LT)
    second = jax.random.randint(second_key, (blocks,), 0, LT)
    counts = 1 + first * second // LT
    busiest = jax.random.randint(third_key, (), 0, blocks)
    counts = jnp.where(jnp.arange(blocks) == busiest, LT, counts)
    return counts.astype(jnp.int32)


def levels(own_key, shape, cuts, low, largest):
    loudness = 1.0
    for dim, parts in cuts:
        steps = jax.random.uniform(jax.random.fold_in(jax.random.fold_in(own_key, 6), dim), (parts,), jnp.float32, low / len(cuts), largest / len(cuts))
        loudness = loudness * jnp.repeat(jnp.exp(steps), shape[dim] // parts).reshape((-1,) + (1,) * (len(shape) - 1 - dim))
    return loudness


def scatter_about(rng, dims, deviation, reach, shards=(), kind=jnp.bfloat16):
    values = deviation * jax.random.normal(rng, dims, jnp.float32)
    if shards:
        values = values * levels(rng, dims, shards, -0.22, 0.18)
    return jnp.clip(values, -reach, reach).astype(kind)


def setup_inputs(seed: int = 0) -> dict:
    key_of = jax.random.split(jax.random.key(seed), 8)
    return {
        "features_t": scatter_about(key_of[0], (F, NODES), 1.0, 6.0, ((0, 4), (1, 128))),
        "tile_values": scatter_about(key_of[1], (LT * N_ROW, TILE, TILE), (TILE * LT // 4) ** -0.5, 0.09375, ((0, 128),)),
        "tile_rows": draw_tile_rows(jax.random.fold_in(key_of[7], 71), 0),
        "tile_cols": draw_tile_cols(jax.random.fold_in(key_of[7], 71), 0),
        "tile_count": draw_tile_count(jax.random.fold_in(key_of[7], 71), 0),
        "weight": scatter_about(key_of[5], (F, HID), F ** -0.5, 0.5),
        "cotangent": scatter_about(key_of[6], (NODES, HID), (1.0 / NODES ** 0.5), 0.078125, ((0, 128), (1, 4))),
    }


def reference(features_t, tile_values, tile_rows, tile_cols, tile_count, weight, cotangent):
    blocks = NTILES // TROWS
    feature_table = features_t.astype(jnp.float32).reshape(F, NTILES, TILE)

    def one_block(block_index):
        start = block_index * LT
        tile_block = lax.dynamic_slice_in_dim(tile_values, start, LT, 0).astype(jnp.float32)
        rows_here = lax.dynamic_slice_in_dim(tile_rows, start, LT, 0)
        cols_here = lax.dynamic_slice_in_dim(tile_cols, start, LT, 0)
        live_count = lax.dynamic_index_in_dim(tile_count, block_index, 0, keepdims=False)
        live_slots = (jnp.arange(LT, dtype=jnp.int32) < live_count).astype(jnp.float32)
        picked = jnp.take(feature_table, cols_here, axis=1)
        terms = jnp.einsum("fsk,sdk->sfd", picked, tile_block, precision=lax.Precision.HIGHEST)
        row_select = (rows_here[:, None] == jnp.arange(TROWS, dtype=jnp.int32)[None, :]).astype(jnp.float32)
        row_select = row_select * live_slots[:, None]
        summed = jnp.einsum("sfd,st->ftd", terms, row_select, precision=lax.Precision.HIGHEST)
        return summed.reshape(F, TROWS * TILE)

    stacked = lax.map(one_block, jnp.arange(blocks, dtype=jnp.int32))
    aggregated = jnp.transpose(stacked, (1, 0, 2)).reshape(F, NODES).astype(jnp.bfloat16)
    pre = jnp.dot(aggregated.T, weight, preferred_element_type=jnp.float32)
    hidden = jax.nn.silu(pre).astype(jnp.bfloat16)
    sigmoid_part = jax.nn.sigmoid(pre)
    slope_term = sigmoid_part + pre * sigmoid_part * (1.0 - sigmoid_part)
    d_pre = (cotangent.astype(jnp.float32) * slope_term).astype(jnp.bfloat16)
    d_weight = jnp.dot(aggregated, d_pre, preferred_element_type=jnp.float32)
    return hidden, d_weight
```

```python
import functools

import jax
import jax.numpy as jnp
from jax import lax
from jax.experimental import pallas as pl
from jax.experimental.pallas import tpu as pltpu
from jax.sharding import PartitionSpec as P

MESH = pl.DeviceIdType.MESH
NY, NX, NZ, NREP = 8, 2, 8, 4
RING = 8
GROUP = 16
SUB = 4
PER = GROUP // SUB
STEPS = (RING // 2 - 1) * SUB + SUB // 2
TILE = 128
SLOTS = 128
BATCH = 8


def kernel(
    rows_ref, cols_ref, count_ref, feat_ref, tv_hbm, weight_ref, cot_ref,
    hidden_ref, dw_ref,
    table, tv, index_s, own, cot_all, agg_all, w_t, rs_src, rs_buf, mid_src, mid_buf, end_buf,
    tv_sem, first_send, first_recv, ring_send, ring_recv,
    cot_send, cot_recv, agg_send, agg_recv,
    rs_send, rs_recv, mid_send, mid_recv, end_send, end_recv,
):
    row = lax.axis_index("row")
    rep = lax.axis_index("rep")
    y = row // (NX * NZ)
    xh = (row // NZ) % NX
    z = row % NZ

    def at(y_, x_, z_):
        return (y_ * NX + x_) * NZ + z_

    def y_peer(p):
        return at((y + p // NX) % NY, (xh + p % NX) % NX, z)

    def z_peer(p):
        return at(y, (xh + p % NX) % NX, (z + p // NX) % NZ)

    barrier = pltpu.get_barrier_semaphore()

    @pl.loop(1, GROUP)
    def _(p):
        pl.semaphore_signal(barrier, inc=1, device_id=(y_peer(p), rep), device_id_type=MESH)
        pl.semaphore_signal(barrier, inc=1, device_id=(z_peer(p), rep), device_id_type=MESH)

    @pl.loop(1, NREP)
    def _(p):
        pl.semaphore_signal(barrier, inc=1, device_id=(row, (rep + p) % NREP), device_id_type=MESH)

    load = pltpu.make_async_copy(tv_hbm, tv, tv_sem)
    load.start()
    own[0] = feat_ref[:, :TILE]
    own[1] = feat_ref[:, TILE:]
    g_y = y * NX + xh
    g_z = z * NX + xh
    place_a = z * GROUP + g_y
    place_b = RING * GROUP + y * GROUP + g_z
    pltpu.make_async_copy(own.at[0], table.at[place_a], first_recv.at[0, g_y // PER]).start()
    pltpu.make_async_copy(own.at[1], table.at[place_b], first_recv.at[1, g_z // PER]).start()
    cot_all[rep] = cot_ref[...]
    pl.semaphore_wait(barrier, 2 * (GROUP - 1) + NREP - 1)

    @pl.loop(1, GROUP)
    def _(p):
        pltpu.make_async_remote_copy(
            src_ref=own.at[0], dst_ref=table.at[place_a],
            send_sem=first_send.at[0], recv_sem=first_recv.at[0, g_y // PER],
            device_id=(y_peer(p), rep), device_id_type=MESH,
        ).start()
        pltpu.make_async_remote_copy(
            src_ref=own.at[1], dst_ref=table.at[place_b],
            send_sem=first_send.at[1], recv_sem=first_recv.at[1, g_z // PER],
            device_id=(z_peer(p), rep), device_id_type=MESH,
        ).start()

    @pl.loop(1, NREP)
    def _(p):
        pltpu.make_async_remote_copy(
            src_ref=cot_all.at[rep], dst_ref=cot_all.at[rep],
            send_sem=cot_send, recv_sem=cot_recv,
            device_id=(row, (rep + p) % NREP), device_id_type=MESH,
        ).start()

    w_t[...] = weight_ref[...].astype(jnp.float32).T.astype(jnp.bfloat16)

    @pl.loop(0, SLOTS)
    def _(s):
        col = cols_ref[s]
        odd = col % 2
        blk = col // 2
        by = blk // (NX * NZ)
        bx = (blk // NZ) % NX
        bz = blk % NZ
        place = jnp.where(
            odd == 0, bz * GROUP + by * NX + bx, RING * GROUP + by * GROUP + bz * NX + bx
        )
        index_s[s] = place

    def waits(ref, sem):
        pltpu.make_async_copy(ref, ref, sem).wait()

    def stream(k):
        half, side = k // 2, k % 2
        sign = 1 - 2 * side
        mine = z if half == 0 else y
        if half == 0:
            to = at(y, xh, (z + sign + NZ) % NZ)
        else:
            to = at((y + sign + NY) % NY, xh, z)
        return half, side, sign, mine, to

    def piece(k, i, shift):
        half, side, sign, mine, _ = stream(k)
        step = i // SUB
        q = i % SUB
        q = jnp.where(step == RING // 2 - 1, q + (SUB // 2) * side, q)
        grp = (mine - sign * (step + shift) + 2 * RING) % RING
        return table.at[pl.ds(half * RING * GROUP + grp * GROUP + q * PER, PER)]

    def send(k, i):
        to = stream(k)[4]
        ref = piece(k, i, 0)
        pltpu.make_async_remote_copy(
            src_ref=ref, dst_ref=ref,
            send_sem=ring_send.at[k], recv_sem=ring_recv.at[k, i],
            device_id=(to, rep), device_id_type=MESH,
        ).start()

    @pl.loop(0, SUB)
    def _(i):
        for half in range(2):
            waits(piece(2 * half, i, 0), first_recv.at[half, i])
            send(2 * half, i)
            send(2 * half + 1, i)

    last = SUB * (RING // 2 - 1)

    @pl.loop(SUB, last)
    def _(i):
        for k in range(4):
            waits(piece(k, i, 0), ring_recv.at[k, i - SUB])
            send(k, i)

    for i in range(last, last + SUB):
        for k in range(4):
            side = k % 2
            waits(piece(k, i - SUB, 1), ring_recv.at[k, i - SUB])
            j = i - (SUB // 2) * side
            if last <= j < STEPS:
                send(k, j)
    for i in range(last, STEPS):
        for k in range(4):
            waits(piece(k, i, 1), ring_recv.at[k, i])

    load.wait()
    count = count_ref[0]

    def batch(b, acc):
        picks = []
        for j in range(BATCH):
            s = b * BATCH + j
            tile = table[index_s[s]]
            live = s < count
            r = rows_ref[s]
            zero = jnp.zeros_like(tile)
            up = jnp.where(live & (r == 0), tile, zero)
            down = jnp.where(live & (r == 1), tile, zero)
            picks.append(jnp.concatenate([up, down], axis=0))
        lhs = jnp.concatenate(picks, axis=1)
        rhs = jnp.concatenate([tv[b * BATCH + j] for j in range(BATCH)], axis=1)
        return acc + lax.dot_general(
            lhs, rhs, (((1,), (1,)), ((), ())), preferred_element_type=jnp.float32
        )

    acc = lax.fori_loop(0, SLOTS // BATCH, batch, jnp.zeros((64, TILE), jnp.float32))
    agg = jnp.concatenate([acc[:32], acc[32:]], axis=1).astype(jnp.bfloat16)
    agg_all[rep] = agg

    @pl.loop(1, NREP)
    def _(p):
        pltpu.make_async_remote_copy(
            src_ref=agg_all.at[rep], dst_ref=agg_all.at[rep],
            send_sem=agg_send, recv_sem=agg_recv,
            device_id=(row, (rep + p) % NREP), device_id_type=MESH,
        ).start()

    three = pl.ds(0, NREP - 1)
    waits(cot_all.at[three], cot_recv)
    waits(agg_all.at[three], agg_recv)

    full = agg_all[...].reshape(4 * 32, 2 * TILE)
    pre_t = jnp.dot(w_t[...], full, preferred_element_type=jnp.float32)
    gate = jax.nn.sigmoid(pre_t)
    slope = gate + pre_t * gate * (1.0 - gate)
    cot = cot_all[...].reshape(4 * 64, 2 * TILE).astype(jnp.float32)
    d_pre_t = (cot * slope).astype(jnp.bfloat16)
    grad = lax.dot_general(
        agg, d_pre_t, (((1,), (1,)), ((), ())), preferred_element_type=jnp.float32
    )
    for j in range(8):
        rs_src[j] = grad[8 * (j // 2):8 * (j // 2) + 8, TILE * (j % 2):TILE * (j % 2) + TILE]
    rs_buf[y] = rs_src[y]

    @pl.loop(1, NY)
    def _(p):
        other = (y + p) % NY
        pltpu.make_async_remote_copy(
            src_ref=rs_src.at[other], dst_ref=rs_buf.at[y],
            send_sem=rs_send, recv_sem=rs_recv,
            device_id=(at(other, xh, z), rep), device_id_type=MESH,
        ).start()

    own_t = jnp.dot(
        w_t[pl.ds(pl.multiple_of(rep * 64, 64), 64), :], full, preferred_element_type=jnp.float32
    )
    hidden_t = own_t * jax.nn.sigmoid(own_t)
    hidden_ref[...] = hidden_t.astype(jnp.bfloat16)

    waits(rs_buf.at[pl.ds(0, NY - 1)], rs_recv)
    total = rs_buf[0]
    for j in range(1, NY):
        total = total + rs_buf[j]
    mid_src[...] = total
    mid_buf[g_z] = total

    @pl.loop(1, GROUP)
    def _(p):
        pltpu.make_async_remote_copy(
            src_ref=mid_src, dst_ref=mid_buf.at[g_z],
            send_sem=mid_send, recv_sem=mid_recv,
            device_id=(z_peer(p), rep), device_id_type=MESH,
        ).start()

    waits(mid_buf.at[pl.ds(0, GROUP - 1)], mid_recv)
    total = mid_buf[0]
    for j in range(1, GROUP):
        total = total + mid_buf[j]
    end_buf[y] = total

    @pl.loop(1, NY)
    def _(p):
        pltpu.make_async_remote_copy(
            src_ref=end_buf.at[y], dst_ref=end_buf.at[y],
            send_sem=end_send, recv_sem=end_recv,
            device_id=(at((y + p) % NY, xh, z), rep), device_id_type=MESH,
        ).start()

    waits(end_buf.at[pl.ds(0, NY - 1)], end_recv)
    for j in range(8):
        dw_ref[8 * (j // 2):8 * (j // 2) + 8, TILE * (j % 2):TILE * (j % 2) + TILE] = end_buf[j]

    for half in range(2):
        waits(table.at[pl.ds(0, GROUP - 1)], first_send.at[half])
    for k in range(4):
        waits(table.at[pl.ds(0, STEPS * PER)], ring_send.at[k])
    waits(cot_all.at[three], cot_send)
    waits(agg_all.at[three], agg_send)
    waits(rs_buf.at[pl.ds(0, NY - 1)], rs_send)
    waits(mid_buf.at[pl.ds(0, GROUP - 1)], mid_send)
    waits(end_buf.at[pl.ds(0, NY - 1)], end_send)


def shards(features_t, tile_values, tile_rows, tile_cols, tile_count, weight, cotangent):
    vmem = pl.BlockSpec(memory_space=pltpu.VMEM)
    smem = pl.BlockSpec(memory_space=pltpu.SMEM)
    dma = pltpu.SemaphoreType.DMA
    bf16, f32 = jnp.bfloat16, jnp.float32
    hidden_t, d_weight = pl.pallas_call(
        kernel,
        out_shape=(
            jax.ShapeDtypeStruct((64, 256), bf16),
            jax.ShapeDtypeStruct((32, 256), f32),
        ),
        in_specs=[smem, smem, smem, vmem, pl.BlockSpec(memory_space=pl.ANY), vmem, vmem],
        out_specs=(vmem, vmem),
        scratch_shapes=[
            pltpu.VMEM((2 * RING * GROUP, 32, TILE), bf16),
            pltpu.VMEM((SLOTS, TILE, TILE), bf16),
            pltpu.SMEM((SLOTS,), jnp.int32),
            pltpu.VMEM((2, 32, TILE), bf16),
            pltpu.VMEM((NREP, 64, 256), bf16),
            pltpu.VMEM((NREP, 32, 256), bf16),
            pltpu.VMEM((256, 128), bf16),
            pltpu.VMEM((8, 8, TILE), f32),
            pltpu.VMEM((8, 8, TILE), f32),
            pltpu.VMEM((8, TILE), f32),
            pltpu.VMEM((GROUP, 8, TILE), f32),
            pltpu.VMEM((8, 8, TILE), f32),
            dma(()), dma((2,)), dma((2, SUB)), dma((4,)), dma((4, STEPS)),
            dma(()), dma(()), dma(()), dma(()),
            dma(()), dma(()), dma(()), dma(()), dma(()), dma(()),
        ],
        compiler_params=pltpu.CompilerParams(
            collective_id=0, has_side_effects=True, vmem_limit_bytes=56 * 1024 * 1024
        ),
        name="layer",
    )(tile_rows, tile_cols, tile_count, features_t, tile_values, weight, cotangent.T)
    return hidden_t.T, d_weight


def solution(mesh):
    placed = (
        P("rep", "row"),
        P("row", None, None),
        P("row"),
        P("row"),
        P("row"),
        P(),
        P("row", "rep"),
    )
    return jax.shard_map(
        shards,
        mesh=mesh,
        in_specs=placed,
        out_specs=(P("row", "rep"), P("rep", None)),
        check_vma=False,
    )
```

```python
import jax
import jax.numpy as jnp
from jax import lax
from jax.experimental import pallas as pl
from jax.experimental.pallas import tpu as pltpu
from jax.sharding import PartitionSpec as P

MESH = pl.DeviceIdType.MESH
NY, NX, NZ, NREP = 8, 2, 8, 4
RING = 8
GROUP = 16
SUB = 8
PER = GROUP // SUB
STEPS = (RING // 2 - 1) * SUB + SUB // 2
TILE = 128
SLOTS = 128
BATCH = 8


def rank(d):
    return jnp.where(d == 0, 0, jnp.where(d <= RING // 2, 2 * d - 1, 2 * (RING - d)))


def far_first(k):
    return RING // 2 + ((k + 1) // 2) * (1 - 2 * (k % 2))


def kernel(
    rows_hbm, cols_hbm, count_hbm, feat_hbm, tv_hbm, weight_hbm, cot_hbm,
    hidden_ref, dw_ref,
    rows_ref, cols_ref, count_ref, index_s, code_s,
    table, tv, weight, cot_all, agg_all, w_t, rs_src, rs_buf, mid_src, mid_buf, end_buf,
    tv_sem, in_sem, x_send, first_send, first_recv, ring_send, ring_recv,
    cot_send, cot_recv, agg_send, agg_recv,
    rs_send, rs_recv, mid_send, mid_recv, end_send, end_recv,
):
    row = lax.axis_index("row")
    rep = lax.axis_index("rep")
    y = row // (NX * NZ)
    xh = (row // NZ) % NX
    z = row % NZ

    def at(y_, x_, z_):
        return (y_ * NX + x_) * NZ + z_

    def y_peer(d):
        return at((y + d) % NY, xh, z)

    def z_peer(d):
        return at(y, xh, (z + d) % NZ)

    def peer(half, d):
        return y_peer(d) if half == 0 else z_peer(d)

    other_x = at(y, 1 - xh, z)

    def waits(ref, sem):
        pltpu.make_async_copy(ref, ref, sem).wait()

    def put(src, dst, send_sem, recv_sem, to, rep_to=None):
        pltpu.make_async_remote_copy(
            src_ref=src, dst_ref=dst, send_sem=send_sem, recv_sem=recv_sem,
            device_id=(to, rep if rep_to is None else rep_to), device_id_type=MESH,
        ).start()

    barrier = pltpu.get_barrier_semaphore()

    def greet(to, rep_to):
        pl.semaphore_signal(barrier, inc=1, device_id=(to, rep_to), device_id_type=MESH)

    @pl.loop(0, RING - 1)
    def _(k):
        greet(y_peer(far_first(k)), rep)
        greet(z_peer(far_first(k)), rep)

    greet(other_x, rep)

    @pl.loop(1, NREP)
    def _(p):
        greet(row, (rep + p) % NREP)

    base = (z * GROUP, RING * GROUP + y * GROUP)
    ins = [
        pltpu.make_async_copy(feat_hbm.at[:, pl.ds(0, TILE)], table.at[base[0]], in_sem.at[0]),
        pltpu.make_async_copy(feat_hbm.at[:, pl.ds(TILE, TILE)], table.at[base[1]], in_sem.at[1]),
        pltpu.make_async_copy(cot_hbm, cot_all.at[rep], in_sem.at[2]),
        pltpu.make_async_copy(weight_hbm, weight, in_sem.at[3]),
        pltpu.make_async_copy(rows_hbm, rows_ref, in_sem.at[4]),
        pltpu.make_async_copy(cols_hbm, cols_ref, in_sem.at[5]),
        pltpu.make_async_copy(count_hbm, count_ref, in_sem.at[6]),
    ]
    for c in ins:
        c.start()
    load = pltpu.make_async_copy(tv_hbm, tv, tv_sem)
    load.start()
    ins[0].wait()
    ins[1].wait()
    pl.semaphore_wait(barrier, 2 * (RING - 1) + 1 + NREP - 1)

    for half in range(2):
        put(table.at[base[half]], table.at[base[half] + 1], x_send.at[half],
            first_recv.at[half, 0], other_x)

    def spread(j, sem):
        @pl.loop(0, RING - 1)
        def _(k):
            d = far_first(k)
            r = rank(RING - d)
            for half in range(2):
                put(table.at[base[half] + j], table.at[base[half] + 2 * r + j],
                    first_send.at[half], first_recv.at[half, r], peer(half, d))

    spread(0, 0)
    ins[2].wait()

    @pl.loop(1, NREP)
    def _(p):
        put(cot_all.at[rep], cot_all.at[rep], cot_send, cot_recv, row, (rep + p) % NREP)

    for half in range(2):
        waits(table.at[0], first_recv.at[half, 0])
    spread(1, 1)

    def piece(k, i, shift):
        half, side = k // 2, k % 2
        sign = 1 - 2 * side
        mine = z if half == 0 else y
        step = i // SUB
        q = i % SUB
        q = jnp.where(step == RING // 2 - 1, q + (SUB // 2) * side, q)
        grp = (mine - sign * (step + shift) + 2 * RING) % RING
        return table.at[pl.ds(half * RING * GROUP + grp * GROUP + q * PER, PER)]

    def send(k, i):
        half, sign = k // 2, 1 - 2 * (k % 2)
        ref = piece(k, i, 0)
        put(ref, ref, ring_send.at[k], ring_recv.at[k, i], peer(1 - half, sign + RING))

    for k in range(4):
        send(k, 0)

    @pl.loop(1, SUB)
    def _(i):
        for half in range(2):
            waits(piece(2 * half, i, 0), first_recv.at[half, i])
            send(2 * half, i)
            send(2 * half + 1, i)

    last = SUB * (RING // 2 - 1)

    @pl.loop(SUB, last)
    def _(i):
        for k in range(4):
            waits(piece(k, i, 0), ring_recv.at[k, i - SUB])
            send(k, i)

    @pl.loop(last, STEPS)
    def _(i):
        for k in (0, 2):
            waits(piece(k, i - SUB, 1), ring_recv.at[k, i - SUB])
            send(k, i)
        for k in (1, 3):
            waits(piece(k, i - SUB, 1), ring_recv.at[k, i - SUB])

    @pl.loop(last, STEPS)
    def _(i):
        for k in (0, 2):
            waits(piece(k, i - SUB // 2, 1), ring_recv.at[k, i - SUB // 2])
        for k in (1, 3):
            waits(piece(k, i - SUB // 2, 1), ring_recv.at[k, i - SUB // 2])
            send(k, i)

    for c in ins[3:]:
        c.wait()
    w_t[...] = weight[...].astype(jnp.float32).T.astype(jnp.bfloat16)
    count = count_ref[0]

    @pl.loop(0, SLOTS)
    def _(s):
        col = cols_ref[s]
        blk = col // 2
        by = blk // (NX * NZ)
        dx = ((blk // NZ) + xh) % NX
        bz = blk % NZ
        place_a = bz * GROUP + rank((by - y + NY) % NY) * 2 + dx
        place_b = RING * GROUP + by * GROUP + rank((bz - z + NZ) % NZ) * 2 + dx
        index_s[s] = jnp.where(col % 2 == 0, place_a, place_b)
        code_s[s] = jnp.where(s < count, rows_ref[s], 2)

    @pl.loop(last, STEPS)
    def _(i):
        for k in range(4):
            waits(piece(k, i, 1), ring_recv.at[k, i])

    load.wait()

    def batch(b, acc):
        picks = []
        for j in range(BATCH):
            s = b * BATCH + j
            tile = table[index_s[s]]
            r = code_s[s]
            zero = jnp.zeros_like(tile)
            up = jnp.where(r == 0, tile, zero)
            down = jnp.where(r == 1, tile, zero)
            picks.append(jnp.concatenate([up, down], axis=0))
        lhs = jnp.concatenate(picks, axis=1)
        rhs = jnp.concatenate([tv[b * BATCH + j] for j in range(BATCH)], axis=1)
        return acc + lax.dot_general(
            lhs, rhs, (((1,), (1,)), ((), ())), preferred_element_type=jnp.float32
        )

    acc = lax.fori_loop(0, SLOTS // BATCH, batch, jnp.zeros((64, TILE), jnp.float32))
    agg = jnp.concatenate([acc[:32], acc[32:]], axis=1).astype(jnp.bfloat16)
    agg_all[rep] = agg

    @pl.loop(1, NREP)
    def _(p):
        put(agg_all.at[rep], agg_all.at[rep], agg_send, agg_recv, row, (rep + p) % NREP)

    three = pl.ds(0, NREP - 1)
    waits(cot_all.at[three], cot_recv)
    waits(agg_all.at[three], agg_recv)

    full = agg_all[...].reshape(4 * 32, 2 * TILE)
    pre_t = jnp.dot(w_t[...], full, preferred_element_type=jnp.float32)
    gate = jax.nn.sigmoid(pre_t)
    slope = gate + pre_t * gate * (1.0 - gate)
    cot = cot_all[...].reshape(4 * 64, 2 * TILE).astype(jnp.float32)
    d_pre_t = (cot * slope).astype(jnp.bfloat16)
    grad = lax.dot_general(
        agg, d_pre_t, (((1,), (1,)), ((), ())), preferred_element_type=jnp.float32
    )
    for j in range(8):
        rs_src[j] = grad[8 * (j // 2):8 * (j // 2) + 8, TILE * (j % 2):TILE * (j % 2) + TILE]

    @pl.loop(0, NY - 1)
    def _(k):
        other = (y + far_first(k)) % NY
        put(rs_src.at[other], rs_buf.at[y], rs_send, rs_recv, at(other, xh, z))

    rs_buf[y] = rs_src[y]

    own_t = jnp.dot(
        w_t[pl.ds(pl.multiple_of(rep * 64, 64), 64), :], full, preferred_element_type=jnp.float32
    )
    hidden_ref[...] = (own_t * jax.nn.sigmoid(own_t)).astype(jnp.bfloat16)

    seven = pl.ds(0, RING - 1)
    waits(rs_buf.at[seven], rs_recv)
    total = rs_buf[0]
    for j in range(1, NY):
        total = total + rs_buf[j]
    mid_src[...] = total
    g_z = z * NX + xh

    @pl.loop(0, RING - 1)
    def _(k):
        z_to = (z + far_first(k)) % NZ
        put(mid_src, mid_buf.at[g_z], mid_send, mid_recv, at(y, 1 - xh, z_to))
        put(mid_src, mid_buf.at[g_z], mid_send, mid_recv, at(y, xh, z_to))

    put(mid_src, mid_buf.at[g_z], mid_send, mid_recv, other_x)
    mid_buf[g_z] = total

    fifteen = pl.ds(0, GROUP - 1)
    waits(mid_buf.at[fifteen], mid_recv)
    total = mid_buf[0]
    for j in range(1, GROUP):
        total = total + mid_buf[j]
    end_buf[y] = total

    @pl.loop(0, RING - 1)
    def _(k):
        put(end_buf.at[y], end_buf.at[y], end_send, end_recv, y_peer(far_first(k)))

    waits(end_buf.at[seven], end_recv)
    for j in range(8):
        dw_ref[8 * (j // 2):8 * (j // 2) + 8, TILE * (j % 2):TILE * (j % 2) + TILE] = end_buf[j]

    for half in range(2):
        waits(table.at[0], x_send.at[half])
        waits(table.at[pl.ds(0, 2 * (RING - 1))], first_send.at[half])
    for k in range(4):
        waits(table.at[pl.ds(0, STEPS * PER)], ring_send.at[k])
    waits(cot_all.at[three], cot_send)
    waits(agg_all.at[three], agg_send)
    waits(rs_buf.at[seven], rs_send)
    waits(mid_buf.at[fifteen], mid_send)
    waits(end_buf.at[seven], end_send)


def shards(features_t, tile_values, tile_rows, tile_cols, tile_count, weight, cotangent):
    vmem = pl.BlockSpec(memory_space=pltpu.VMEM)
    hbm = pl.BlockSpec(memory_space=pl.ANY)
    dma = pltpu.SemaphoreType.DMA
    bf16, f32 = jnp.bfloat16, jnp.float32
    hidden_t, d_weight = pl.pallas_call(
        kernel,
        out_shape=(
            jax.ShapeDtypeStruct((64, 256), bf16),
            jax.ShapeDtypeStruct((32, 256), f32),
        ),
        in_specs=[hbm] * 7,
        out_specs=(vmem, vmem),
        scratch_shapes=[
            pltpu.SMEM((SLOTS,), jnp.int32),
            pltpu.SMEM((SLOTS,), jnp.int32),
            pltpu.SMEM((1,), jnp.int32),
            pltpu.SMEM((SLOTS,), jnp.int32),
            pltpu.SMEM((SLOTS,), jnp.int32),
            pltpu.VMEM((2 * RING * GROUP, 32, TILE), bf16),
            pltpu.VMEM((SLOTS, TILE, TILE), bf16),
            pltpu.VMEM((128, 256), bf16),
            pltpu.VMEM((NREP, 64, 256), bf16),
            pltpu.VMEM((NREP, 32, 256), bf16),
            pltpu.VMEM((256, 128), bf16),
            pltpu.VMEM((8, 8, TILE), f32),
            pltpu.VMEM((8, 8, TILE), f32),
            pltpu.VMEM((8, TILE), f32),
            pltpu.VMEM((GROUP, 8, TILE), f32),
            pltpu.VMEM((8, 8, TILE), f32),
            dma(()), dma((7,)), dma((2,)), dma((2,)), dma((2, SUB)), dma((4,)), dma((4, STEPS)),
            dma(()), dma(()), dma(()), dma(()),
            dma(()), dma(()), dma(()), dma(()), dma(()), dma(()),
        ],
        compiler_params=pltpu.CompilerParams(
            collective_id=0, has_side_effects=True, vmem_limit_bytes=56 * 1024 * 1024
        ),
        name="layer",
    )(tile_rows, tile_cols, tile_count, features_t, tile_values, weight, cotangent.T)
    return hidden_t.T, d_weight


def solution(mesh):
    placed = (
        P("rep", "row"),
        P("row", None, None),
        P("row"),
        P("row"),
        P("row"),
        P(),
        P("row", "rep"),
    )
    return jax.shard_map(
        shards,
        mesh=mesh,
        in_specs=placed,
        out_specs=(P("row", "rep"), P("rep", None)),
        check_vma=False,
    )
```

```python
import jax
import jax.numpy as jnp
from jax import lax
from jax.experimental import pallas as pl
from jax.experimental.pallas import tpu as pltpu
from jax.sharding import PartitionSpec as P

MESH = pl.DeviceIdType.MESH
NY, NX, NZ, NREP = 8, 2, 8, 4
RING = 8
GROUP = 16
SUB = 8
LEAD = 5
PER = GROUP // SUB
TILE = 128
SLOTS = 128
BATCH = 8


def mod(a, n):
    return lax.rem(a, jnp.int32(n))


def rank(d):
    return jnp.where(d == 0, 0, jnp.where(d <= RING // 2, 2 * d - 1, 2 * (RING - d)))


def far_first(k):
    return RING // 2 + lax.div(k + 1, jnp.int32(2)) * (1 - 2 * mod(k, 2))


def kernel(
    rows_hbm, cols_hbm, count_hbm, feat_hbm, tv_hbm, weight_hbm, cot_hbm,
    hidden_ref, dw_ref,
    rows_ref, cols_ref, count_ref, index_s, code_s,
    table, tv, weight, cot_all, agg_all, w_t, rs_src, rs_buf, mid_src, mid_buf, end_buf,
    tv_sem, in_sem, first_send, first_recv, ring_send, two_recv, rest_recv,
    cot_send, cot_recv, agg_send, agg_recv,
    rs_send, rs_recv, mid_send, mid_recv, end_send, end_recv,
):
    row = lax.axis_index("row")
    rep = lax.axis_index("rep")
    y = lax.div(row, jnp.int32(NX * NZ))
    xh = mod(lax.div(row, jnp.int32(NZ)), NX)
    z = mod(row, NZ)

    def at(y_, x_, z_):
        return (y_ * NX + x_) * NZ + z_

    def peer(half, d, dx=0):
        x_ = mod(xh + dx, NX)
        return at(mod(y + d, NY), x_, z) if half == 0 else at(y, x_, mod(z + d, NZ))

    def waits(ref, sem):
        pltpu.make_async_copy(ref, ref, sem).wait()

    def put(src, dst, send_sem, recv_sem, to, rep_to=None):
        pltpu.make_async_remote_copy(
            src_ref=src, dst_ref=dst, send_sem=send_sem, recv_sem=recv_sem,
            device_id=(to, rep if rep_to is None else rep_to), device_id_type=MESH,
        ).start()

    barrier = pltpu.get_barrier_semaphore()

    def greet(to, rep_to):
        pl.semaphore_signal(barrier, inc=1, device_id=(to, rep_to), device_id_type=MESH)

    @pl.loop(0, RING - 1)
    def _(k):
        d = far_first(k)
        for half in range(2):
            greet(peer(half, d, 1), rep)
            greet(peer(half, d), rep)

    for half in range(2):
        greet(peer(half, 0, 1), rep)

    @pl.loop(1, NREP)
    def _(p):
        greet(row, mod(rep + p, NREP))

    base = (z * GROUP, RING * GROUP + y * GROUP)
    ins = [
        pltpu.make_async_copy(feat_hbm.at[:, pl.ds(0, TILE)], table.at[base[0]], in_sem.at[0]),
        pltpu.make_async_copy(feat_hbm.at[:, pl.ds(TILE, TILE)], table.at[base[1]], in_sem.at[1]),
        pltpu.make_async_copy(cot_hbm, cot_all.at[rep], in_sem.at[2]),
        pltpu.make_async_copy(weight_hbm, weight, in_sem.at[3]),
        pltpu.make_async_copy(rows_hbm, rows_ref, in_sem.at[4]),
        pltpu.make_async_copy(cols_hbm, cols_ref, in_sem.at[5]),
        pltpu.make_async_copy(count_hbm, count_ref, in_sem.at[6]),
    ]
    for c in ins:
        c.start()
    load = pltpu.make_async_copy(tv_hbm, tv, tv_sem)
    load.start()
    ins[0].wait()
    ins[1].wait()
    pl.semaphore_wait(barrier, 2 * (GROUP - 1) + NREP - 1)

    def spread(half, d, dx):
        r = rank(mod(RING - d, RING))
        put(table.at[base[half]], table.at[base[half] + 2 * r + dx],
            first_send.at[half], first_recv.at[half, r], peer(half, d, dx))

    for half in range(2):
        spread(half, jnp.int32(0), 1)

    @pl.loop(0, RING - 1)
    def _(k):
        for half in range(2):
            spread(half, far_first(k), 1)
            spread(half, far_first(k), 0)

    ins[2].wait()

    @pl.loop(1, NREP)
    def _(p):
        put(cot_all.at[rep], cot_all.at[rep], cot_send, cot_recv, row, mod(rep + p, NREP))

    mine = (z, y)
    ahead = [
        [[peer(1 - half, RING + sign * d) for d in (1, 2)] for sign in (1, -1)]
        for half in range(2)
    ]
    from_two = [[mod(mine[half] + RING - 2 * sign, RING) for sign in (1, -1)] for half in range(2)]

    def piece(half, grp, q, n=PER):
        return table.at[pl.ds(half * RING * GROUP + grp * GROUP + q * PER, n)]

    def own_piece(q, n=PER):
        for half in range(2):
            waits(piece(half, mine[half], q, n), first_recv.at[half, q])
            ref = piece(half, mine[half], q)
            for side in range(2):
                put(ref, ref, ring_send.at[half, side], two_recv.at[half, side, q],
                    ahead[half][side][1])
                put(ref, ref, ring_send.at[half, side], rest_recv.at[half, side, 0],
                    ahead[half][side][0])

    def pass_piece(q):
        for half in range(2):
            for side in range(2):
                ref = piece(half, from_two[half][side], q)
                waits(ref, two_recv.at[half, side, q])
                put(ref, ref, ring_send.at[half, side], rest_recv.at[half, side, 1],
                    ahead[half][side][0])

                @pl.when(mod(q, 2) == side)
                def _():
                    put(ref, ref, ring_send.at[half, side], rest_recv.at[half, side, 2],
                        ahead[half][side][1])

    own_piece(0, 1)

    @pl.loop(1, LEAD)
    def _(q):
        own_piece(q)

    @pl.loop(LEAD, SUB)
    def _(q):
        own_piece(q)
        pass_piece(q - LEAD)

    @pl.loop(SUB - LEAD, SUB)
    def _(q):
        pass_piece(q)

    for c in ins[3:]:
        c.wait()
    w_t[...] = weight[...].astype(jnp.float32).T.astype(jnp.bfloat16)
    count = count_ref[0]

    @pl.loop(0, SLOTS)
    def _(s):
        col = cols_ref[s]
        blk = lax.div(col, jnp.int32(2))
        by = lax.div(blk, jnp.int32(NX * NZ))
        dx = mod(lax.div(blk, jnp.int32(NZ)) + xh, NX)
        bz = mod(blk, NZ)
        place_a = bz * GROUP + rank(mod(by - y + NY, NY)) * 2 + dx
        place_b = RING * GROUP + by * GROUP + rank(mod(bz - z + NZ, NZ)) * 2 + dx
        index_s[s] = jnp.where(mod(col, 2) == 0, place_a, place_b)
        code_s[s] = jnp.where(s < count, rows_ref[s], 2)

    for kind in range(3):
        for half in range(2):
            for side in range(2):
                waits(table.at[pl.ds(0, (GROUP, GROUP, GROUP // 2)[kind])],
                      rest_recv.at[half, side, kind])

    load.wait()

    def batch(b, acc):
        picks = []
        for j in range(BATCH):
            s = b * BATCH + j
            tile = table[index_s[s]]
            r = code_s[s]
            zero = jnp.zeros_like(tile)
            up = jnp.where(r == 0, tile, zero)
            down = jnp.where(r == 1, tile, zero)
            picks.append(jnp.concatenate([up, down], axis=0))
        lhs = jnp.concatenate(picks, axis=1)
        rhs = jnp.concatenate([tv[b * BATCH + j] for j in range(BATCH)], axis=1)
        return acc + lax.dot_general(
            lhs, rhs, (((1,), (1,)), ((), ())), preferred_element_type=jnp.float32
        )

    acc = lax.fori_loop(0, SLOTS // BATCH, batch, jnp.zeros((64, TILE), jnp.float32))
    agg = jnp.concatenate([acc[:32], acc[32:]], axis=1).astype(jnp.bfloat16)
    agg_all[rep] = agg

    @pl.loop(1, NREP)
    def _(p):
        put(agg_all.at[rep], agg_all.at[rep], agg_send, agg_recv, row, mod(rep + p, NREP))

    three = pl.ds(0, NREP - 1)
    waits(cot_all.at[three], cot_recv)
    waits(agg_all.at[three], agg_recv)

    full = agg_all[...].reshape(4 * 32, 2 * TILE)
    pre_t = jnp.dot(w_t[...], full, preferred_element_type=jnp.float32)
    gate = jax.nn.sigmoid(pre_t)
    slope = gate + pre_t * gate * (1.0 - gate)
    cot = cot_all[...].reshape(4 * 64, 2 * TILE).astype(jnp.float32)
    d_pre_t = (cot * slope).astype(jnp.bfloat16)
    grad = lax.dot_general(
        agg, d_pre_t, (((1,), (1,)), ((), ())), preferred_element_type=jnp.float32
    )
    for j in range(8):
        rs_src[j] = grad[8 * (j // 2):8 * (j // 2) + 8, TILE * (j % 2):TILE * (j % 2) + TILE]

    @pl.loop(0, NY - 1)
    def _(k):
        other = mod(y + far_first(k), NY)
        put(rs_src.at[other], rs_buf.at[y], rs_send, rs_recv, at(other, xh, z))

    rs_buf[y] = rs_src[y]

    own_t = jnp.dot(
        w_t[pl.ds(pl.multiple_of(rep * 64, 64), 64), :], full, preferred_element_type=jnp.float32
    )
    hidden_ref[...] = (own_t * jax.nn.sigmoid(own_t)).astype(jnp.bfloat16)

    seven = pl.ds(0, RING - 1)
    waits(rs_buf.at[seven], rs_recv)
    total = rs_buf[0]
    for j in range(1, NY):
        total = total + rs_buf[j]
    mid_src[...] = total
    g_z = z * NX + xh

    @pl.loop(0, RING - 1)
    def _(k):
        z_to = mod(z + far_first(k), NZ)
        put(mid_src, mid_buf.at[g_z], mid_send, mid_recv, at(y, 1 - xh, z_to))
        put(mid_src, mid_buf.at[g_z], mid_send, mid_recv, at(y, xh, z_to))

    put(mid_src, mid_buf.at[g_z], mid_send, mid_recv, at(y, 1 - xh, z))
    mid_buf[g_z] = total

    fifteen = pl.ds(0, GROUP - 1)
    waits(mid_buf.at[fifteen], mid_recv)
    total = mid_buf[0]
    for j in range(1, GROUP):
        total = total + mid_buf[j]
    end_buf[y] = total

    @pl.loop(0, RING - 1)
    def _(k):
        put(end_buf.at[y], end_buf.at[y], end_send, end_recv, peer(0, far_first(k)))

    waits(end_buf.at[seven], end_recv)
    for j in range(8):
        dw_ref[8 * (j // 2):8 * (j // 2) + 8, TILE * (j % 2):TILE * (j % 2) + TILE] = end_buf[j]

    for half in range(2):
        waits(table.at[pl.ds(0, GROUP - 1)], first_send.at[half])
        for side in range(2):
            waits(table.at[pl.ds(0, 7 * GROUP // 2)], ring_send.at[half, side])
    waits(cot_all.at[three], cot_send)
    waits(agg_all.at[three], agg_send)
    waits(rs_buf.at[seven], rs_send)
    waits(mid_buf.at[fifteen], mid_send)
    waits(end_buf.at[seven], end_send)


def shards(features_t, tile_values, tile_rows, tile_cols, tile_count, weight, cotangent):
    vmem = pl.BlockSpec(memory_space=pltpu.VMEM)
    hbm = pl.BlockSpec(memory_space=pl.ANY)
    dma = pltpu.SemaphoreType.DMA
    bf16, f32 = jnp.bfloat16, jnp.float32
    hidden_t, d_weight = pl.pallas_call(
        kernel,
        out_shape=(
            jax.ShapeDtypeStruct((64, 256), bf16),
            jax.ShapeDtypeStruct((32, 256), f32),
        ),
        in_specs=[hbm] * 7,
        out_specs=(vmem, vmem),
        scratch_shapes=[
            pltpu.SMEM((SLOTS,), jnp.int32),
            pltpu.SMEM((SLOTS,), jnp.int32),
            pltpu.SMEM((1,), jnp.int32),
            pltpu.SMEM((SLOTS,), jnp.int32),
            pltpu.SMEM((SLOTS,), jnp.int32),
            pltpu.VMEM((2 * RING * GROUP, 32, TILE), bf16),
            pltpu.VMEM((SLOTS, TILE, TILE), bf16),
            pltpu.VMEM((128, 256), bf16),
            pltpu.VMEM((NREP, 64, 256), bf16),
            pltpu.VMEM((NREP, 32, 256), bf16),
            pltpu.VMEM((256, 128), bf16),
            pltpu.VMEM((8, 8, TILE), f32),
            pltpu.VMEM((8, 8, TILE), f32),
            pltpu.VMEM((8, TILE), f32),
            pltpu.VMEM((GROUP, 8, TILE), f32),
            pltpu.VMEM((8, 8, TILE), f32),
            dma(()), dma((7,)), dma((2,)), dma((2, SUB)),
            dma((2, 2)), dma((2, 2, SUB)), dma((2, 2, 3)),
            dma(()), dma(()), dma(()), dma(()),
            dma(()), dma(()), dma(()), dma(()), dma(()), dma(()),
        ],
        compiler_params=pltpu.CompilerParams(
            collective_id=0, has_side_effects=True, vmem_limit_bytes=56 * 1024 * 1024
        ),
        name="layer",
    )(tile_rows, tile_cols, tile_count, features_t, tile_values, weight, cotangent.T)
    return hidden_t.T, d_weight


def solution(mesh):
    placed = (
        P("rep", "row"),
        P("row", None, None),
        P("row"),
        P("row"),
        P("row"),
        P(),
        P("row", "rep"),
    )
    return jax.shard_map(
        shards,
        mesh=mesh,
        in_specs=placed,
        out_specs=(P("row", "rep"), P("rep", None)),
        check_vma=False,
    )
```

```python
import jax
import jax.numpy as jnp
from jax import lax
from jax.experimental import pallas as pl
from jax.experimental.pallas import tpu as pltpu
from jax.sharding import PartitionSpec as P

MESH = pl.DeviceIdType.MESH
NY, NX, NZ, NREP = 8, 2, 8, 4
RING = 8
GROUP = 16
SUB = 8
LEAD = 5
PER = GROUP // SUB
TILE = 128
SLOTS = 128
BATCH = 32


def mod(a, n):
    return lax.rem(a, jnp.int32(n))


def rank(d):
    return jnp.where(d == 0, 0, jnp.where(d <= RING // 2, 2 * d - 1, 2 * (RING - d)))


def far_first(k):
    return RING // 2 + lax.div(k + 1, jnp.int32(2)) * (1 - 2 * mod(k, 2))


def kernel(
    rows_hbm, cols_hbm, count_hbm, feat_hbm, tv_hbm, weight_hbm, cot_hbm,
    hidden_ref, dw_ref,
    rows_ref, cols_ref, count_ref, index_s, code_s,
    table, tv, weight, cot_all, agg_all, w_t, rs_src, rs_buf, mid_src, mid_buf, end_buf,
    tv_sem, in_sem, first_send, first_recv, ring_send, two_recv, rest_recv,
    cot_send, cot_recv, agg_send, agg_recv,
    rs_send, rs_recv, mid_send, mid_recv, end_send, end_recv,
):
    row = lax.axis_index("row")
    rep = lax.axis_index("rep")
    y = lax.div(row, jnp.int32(NX * NZ))
    xh = mod(lax.div(row, jnp.int32(NZ)), NX)
    z = mod(row, NZ)

    def at(y_, x_, z_):
        return (y_ * NX + x_) * NZ + z_

    def peer(half, d, dx=0):
        x_ = mod(xh + dx, NX)
        return at(mod(y + d, NY), x_, z) if half == 0 else at(y, x_, mod(z + d, NZ))

    def waits(ref, sem):
        pltpu.make_async_copy(ref, ref, sem).wait()

    def put(src, dst, send_sem, recv_sem, to, rep_to=None):
        pltpu.make_async_remote_copy(
            src_ref=src, dst_ref=dst, send_sem=send_sem, recv_sem=recv_sem,
            device_id=(to, rep if rep_to is None else rep_to), device_id_type=MESH,
        ).start()

    barrier = pltpu.get_barrier_semaphore()

    def greet(to, rep_to):
        pl.semaphore_signal(barrier, inc=1, device_id=(to, rep_to), device_id_type=MESH)

    @pl.loop(0, RING - 1)
    def _(k):
        d = far_first(k)
        for half in range(2):
            greet(peer(half, d, 1), rep)
            greet(peer(half, d), rep)

    for half in range(2):
        greet(peer(half, 0, 1), rep)

    @pl.loop(1, NREP)
    def _(p):
        greet(row, mod(rep + p, NREP))

    base = (z * GROUP, RING * GROUP + y * GROUP)
    ins = [
        pltpu.make_async_copy(feat_hbm.at[:, pl.ds(0, TILE)], table.at[base[0]], in_sem.at[0]),
        pltpu.make_async_copy(feat_hbm.at[:, pl.ds(TILE, TILE)], table.at[base[1]], in_sem.at[1]),
        pltpu.make_async_copy(cot_hbm, cot_all.at[rep], in_sem.at[2]),
        pltpu.make_async_copy(weight_hbm, weight, in_sem.at[3]),
        pltpu.make_async_copy(rows_hbm, rows_ref, in_sem.at[4]),
        pltpu.make_async_copy(cols_hbm, cols_ref, in_sem.at[5]),
        pltpu.make_async_copy(count_hbm, count_ref, in_sem.at[6]),
    ]
    for c in ins:
        c.start()
    load = pltpu.make_async_copy(tv_hbm, tv, tv_sem)
    load.start()
    ins[0].wait()
    ins[1].wait()
    pl.semaphore_wait(barrier, 2 * (GROUP - 1) + NREP - 1)

    def spread(half, d, dx):
        r = rank(mod(RING - d, RING))
        put(table.at[base[half]], table.at[base[half] + 2 * r + dx],
            first_send.at[half], first_recv.at[half, r], peer(half, d, dx))

    for half in range(2):
        spread(half, jnp.int32(0), 1)

    @pl.loop(0, RING - 1)
    def _(k):
        for half in range(2):
            spread(half, far_first(k), 1)
            spread(half, far_first(k), 0)

    ins[2].wait()

    @pl.loop(1, NREP)
    def _(p):
        put(cot_all.at[rep], cot_all.at[rep], cot_send, cot_recv, row, mod(rep + p, NREP))

    mine = (z, y)
    ahead = [
        [[peer(1 - half, RING + sign * d) for d in (1, 2)] for sign in (1, -1)]
        for half in range(2)
    ]
    from_two = [[mod(mine[half] + RING - 2 * sign, RING) for sign in (1, -1)] for half in range(2)]

    def piece(half, grp, q, n=PER):
        return table.at[pl.ds(half * RING * GROUP + grp * GROUP + q * PER, n)]

    def own_piece(q, n=PER):
        for half in range(2):
            waits(piece(half, mine[half], q, n), first_recv.at[half, q])
            ref = piece(half, mine[half], q)
            for side in range(2):
                put(ref, ref, ring_send.at[half, side], two_recv.at[half, side, q],
                    ahead[half][side][1])

    def pass_piece(q):
        for half in range(2):
            for side in range(2):
                ref = piece(half, from_two[half][side], q)
                waits(ref, two_recv.at[half, side, q])
                put(ref, ref, ring_send.at[half, side], rest_recv.at[half, side, 1],
                    ahead[half][side][0])

                @pl.when(mod(q, 2) == side)
                def _():
                    put(ref, ref, ring_send.at[half, side], rest_recv.at[half, side, 2],
                        ahead[half][side][1])

    own_piece(0, 1)

    @pl.loop(1, LEAD)
    def _(q):
        own_piece(q)

    @pl.loop(LEAD, SUB)
    def _(q):
        own_piece(q)
        pass_piece(q - LEAD)

    @pl.loop(SUB - LEAD, SUB)
    def _(q):
        pass_piece(q)

    for half in range(2):
        for side in range(2):
            ref = piece(half, mine[half], 0, GROUP)
            put(ref, ref, ring_send.at[half, side], rest_recv.at[half, side, 0],
                ahead[half][side][0])

    for c in ins[3:]:
        c.wait()
    w_t[...] = weight[...].astype(jnp.float32).T.astype(jnp.bfloat16)
    count = count_ref[0]

    @pl.loop(0, SLOTS)
    def _(s):
        col = cols_ref[s]
        blk = lax.div(col, jnp.int32(2))
        by = lax.div(blk, jnp.int32(NX * NZ))
        dx = mod(lax.div(blk, jnp.int32(NZ)) + xh, NX)
        bz = mod(blk, NZ)
        place_a = bz * GROUP + rank(mod(by - y + NY, NY)) * 2 + dx
        place_b = RING * GROUP + by * GROUP + rank(mod(bz - z + NZ, NZ)) * 2 + dx
        index_s[s] = jnp.where(mod(col, 2) == 0, place_a, place_b)
        code_s[s] = jnp.where(s < count, rows_ref[s], 2)

    for kind in range(3):
        for half in range(2):
            for side in range(2):
                waits(table.at[pl.ds(0, (GROUP, GROUP, GROUP // 2)[kind])],
                      rest_recv.at[half, side, kind])

    load.wait()

    def batch(b, acc):
        picks = []
        for j in range(BATCH):
            s = b * BATCH + j
            tile = table[index_s[s]]
            r = code_s[s]
            zero = jnp.zeros_like(tile)
            up = jnp.where(r == 0, tile, zero)
            down = jnp.where(r == 1, tile, zero)
            picks.append(jnp.concatenate([up, down], axis=0))
        lhs = jnp.concatenate(picks, axis=1)
        rhs = jnp.concatenate([tv[b * BATCH + j] for j in range(BATCH)], axis=1)
        return acc + lax.dot_general(
            lhs, rhs, (((1,), (1,)), ((), ())), preferred_element_type=jnp.float32
        )

    acc = lax.fori_loop(0, SLOTS // BATCH, batch, jnp.zeros((64, TILE), jnp.float32))
    agg = jnp.concatenate([acc[:32], acc[32:]], axis=1).astype(jnp.bfloat16)
    agg_all[rep] = agg

    @pl.loop(1, NREP)
    def _(p):
        put(agg_all.at[rep], agg_all.at[rep], agg_send, agg_recv, row, mod(rep + p, NREP))

    three = pl.ds(0, NREP - 1)
    waits(cot_all.at[three], cot_recv)
    waits(agg_all.at[three], agg_recv)

    full = agg_all[...].reshape(4 * 32, 2 * TILE)
    pre_t = jnp.dot(w_t[...], full, preferred_element_type=jnp.float32)
    gate = jax.nn.sigmoid(pre_t)
    slope = gate + pre_t * gate * (1.0 - gate)
    cot = cot_all[...].reshape(4 * 64, 2 * TILE).astype(jnp.float32)
    d_pre_t = (cot * slope).astype(jnp.bfloat16)
    grad = lax.dot_general(
        agg, d_pre_t, (((1,), (1,)), ((), ())), preferred_element_type=jnp.float32
    )
    for j in range(8):
        rs_src[j] = grad[8 * (j // 2):8 * (j // 2) + 8, TILE * (j % 2):TILE * (j % 2) + TILE]

    @pl.loop(0, NY - 1)
    def _(k):
        other = mod(y + far_first(k), NY)
        put(rs_src.at[other], rs_buf.at[y], rs_send, rs_recv, at(other, xh, z))

    rs_buf[y] = rs_src[y]

    own_t = jnp.dot(
        w_t[pl.ds(pl.multiple_of(rep * 64, 64), 64), :], full, preferred_element_type=jnp.float32
    )
    hidden_ref[...] = (own_t * jax.nn.sigmoid(own_t)).astype(jnp.bfloat16)

    seven = pl.ds(0, RING - 1)
    waits(rs_buf.at[seven], rs_recv)
    total = rs_buf[0]
    for j in range(1, NY):
        total = total + rs_buf[j]
    mid_src[...] = total
    g_z = z * NX + xh

    @pl.loop(0, RING - 1)
    def _(k):
        z_to = mod(z + far_first(k), NZ)
        put(mid_src, mid_buf.at[g_z], mid_send, mid_recv, at(y, 1 - xh, z_to))
        put(mid_src, mid_buf.at[g_z], mid_send, mid_recv, at(y, xh, z_to))

    put(mid_src, mid_buf.at[g_z], mid_send, mid_recv, at(y, 1 - xh, z))
    mid_buf[g_z] = total

    fifteen = pl.ds(0, GROUP - 1)
    waits(mid_buf.at[fifteen], mid_recv)
    total = mid_buf[0]
    for j in range(1, GROUP):
        total = total + mid_buf[j]
    end_buf[y] = total

    @pl.loop(0, RING - 1)
    def _(k):
        put(end_buf.at[y], end_buf.at[y], end_send, end_recv, peer(0, far_first(k)))

    waits(end_buf.at[seven], end_recv)
    for j in range(8):
        dw_ref[8 * (j // 2):8 * (j // 2) + 8, TILE * (j % 2):TILE * (j % 2) + TILE] = end_buf[j]

    for half in range(2):
        waits(table.at[pl.ds(0, GROUP - 1)], first_send.at[half])
        for side in range(2):
            waits(table.at[pl.ds(0, 7 * GROUP // 2)], ring_send.at[half, side])
    waits(cot_all.at[three], cot_send)
    waits(agg_all.at[three], agg_send)
    waits(rs_buf.at[seven], rs_send)
    waits(mid_buf.at[fifteen], mid_send)
    waits(end_buf.at[seven], end_send)


def shards(features_t, tile_values, tile_rows, tile_cols, tile_count, weight, cotangent):
    vmem = pl.BlockSpec(memory_space=pltpu.VMEM)
    hbm = pl.BlockSpec(memory_space=pl.ANY)
    dma = pltpu.SemaphoreType.DMA
    bf16, f32 = jnp.bfloat16, jnp.float32
    hidden_t, d_weight = pl.pallas_call(
        kernel,
        out_shape=(
            pltpu.VMEM((64, 256), bf16),
            pltpu.VMEM((32, 256), f32),
        ),
        in_specs=[hbm] * 7,
        out_specs=(vmem, vmem),
        scratch_shapes=[
            pltpu.SMEM((SLOTS,), jnp.int32),
            pltpu.SMEM((SLOTS,), jnp.int32),
            pltpu.SMEM((1,), jnp.int32),
            pltpu.SMEM((SLOTS,), jnp.int32),
            pltpu.SMEM((SLOTS,), jnp.int32),
            pltpu.VMEM((2 * RING * GROUP, 32, TILE), bf16),
            pltpu.VMEM((SLOTS, TILE, TILE), bf16),
            pltpu.VMEM((128, 256), bf16),
            pltpu.VMEM((NREP, 64, 256), bf16),
            pltpu.VMEM((NREP, 32, 256), bf16),
            pltpu.VMEM((256, 128), bf16),
            pltpu.VMEM((8, 8, TILE), f32),
            pltpu.VMEM((8, 8, TILE), f32),
            pltpu.VMEM((8, TILE), f32),
            pltpu.VMEM((GROUP, 8, TILE), f32),
            pltpu.VMEM((8, 8, TILE), f32),
            dma(()), dma((7,)), dma((2,)), dma((2, SUB)),
            dma((2, 2)), dma((2, 2, SUB)), dma((2, 2, 3)),
            dma(()), dma(()), dma(()), dma(()),
            dma(()), dma(()), dma(()), dma(()), dma(()), dma(()),
        ],
        compiler_params=pltpu.CompilerParams(
            collective_id=0, has_side_effects=True, vmem_limit_bytes=56 * 1024 * 1024
        ),
        name="layer",
    )(tile_rows, tile_cols, tile_count, features_t, tile_values, weight, cotangent.T)
    return hidden_t.T, d_weight


def solution(mesh):
    placed = (
        P("rep", "row"),
        P("row", None, None),
        P("row"),
        P("row"),
        P("row"),
        P(),
        P("row", "rep"),
    )
    return jax.shard_map(
        shards,
        mesh=mesh,
        in_specs=placed,
        out_specs=(P("row", "rep"), P("rep", None)),
        check_vma=False,
    )
```

```python
import jax
import jax.numpy as jnp
from jax import lax
from jax.experimental import pallas as pl
from jax.experimental.pallas import tpu as pltpu
from jax.sharding import PartitionSpec as P

MESH = pl.DeviceIdType.MESH
NY, NX, NZ, NREP = 8, 2, 8, 4
RING = 8
GROUP = 16
SUB = 8
LEAD = 7
PER = GROUP // SUB
TILE = 128
SLOTS = 128
BATCH = 32


def mod(a, n):
    return lax.rem(a, jnp.int32(n))


def rank(d):
    return jnp.where(d == 0, 0, jnp.where(d <= RING // 2, 2 * d - 1, 2 * (RING - d)))


def far_first(k):
    return RING // 2 + lax.div(k + 1, jnp.int32(2)) * (1 - 2 * mod(k, 2))


def kernel(
    rows_hbm, cols_hbm, count_hbm, feat_hbm, tv_hbm, weight_hbm, cot_hbm,
    hidden_ref, dw_ref,
    rows_ref, cols_ref, count_ref, index_s, code_s,
    table, tv, weight, cot_all, agg_all, w_t, rs_src, rs_buf, mid_src, mid_buf, end_buf,
    tv_sem, in_sem, first_send, first_recv, ring_send, two_recv, rest_recv,
    cot_send, cot_recv, agg_send, agg_recv,
    rs_send, rs_recv, mid_send, mid_recv, end_send, end_recv,
):
    row = lax.axis_index("row")
    rep = lax.axis_index("rep")
    y = lax.div(row, jnp.int32(NX * NZ))
    xh = mod(lax.div(row, jnp.int32(NZ)), NX)
    z = mod(row, NZ)

    def at(y_, x_, z_):
        return (y_ * NX + x_) * NZ + z_

    def peer(half, d, dx=0):
        x_ = mod(xh + dx, NX)
        return at(mod(y + d, NY), x_, z) if half == 0 else at(y, x_, mod(z + d, NZ))

    def waits(ref, sem):
        pltpu.make_async_copy(ref, ref, sem).wait()

    def put(src, dst, send_sem, recv_sem, to, rep_to=None):
        pltpu.make_async_remote_copy(
            src_ref=src, dst_ref=dst, send_sem=send_sem, recv_sem=recv_sem,
            device_id=(to, rep if rep_to is None else rep_to), device_id_type=MESH,
        ).start()

    barrier = pltpu.get_barrier_semaphore()

    def greet(to, rep_to):
        pl.semaphore_signal(barrier, inc=1, device_id=(to, rep_to), device_id_type=MESH)

    @pl.loop(0, RING - 1)
    def _(k):
        d = far_first(k)
        for half in range(2):
            greet(peer(half, d, 1), rep)
            greet(peer(half, d), rep)

    for half in range(2):
        greet(peer(half, 0, 1), rep)

    @pl.loop(1, NREP)
    def _(p):
        greet(row, mod(rep + p, NREP))

    base = (z * GROUP, RING * GROUP + y * GROUP)
    ins = [
        pltpu.make_async_copy(feat_hbm.at[:, pl.ds(0, TILE)], table.at[base[0]], in_sem.at[0]),
        pltpu.make_async_copy(feat_hbm.at[:, pl.ds(TILE, TILE)], table.at[base[1]], in_sem.at[1]),
        pltpu.make_async_copy(cot_hbm, cot_all.at[rep], in_sem.at[2]),
        pltpu.make_async_copy(weight_hbm, weight, in_sem.at[3]),
        pltpu.make_async_copy(rows_hbm, rows_ref, in_sem.at[4]),
        pltpu.make_async_copy(cols_hbm, cols_ref, in_sem.at[5]),
        pltpu.make_async_copy(count_hbm, count_ref, in_sem.at[6]),
    ]
    for c in ins:
        c.start()
    load = pltpu.make_async_copy(tv_hbm, tv, tv_sem)
    load.start()
    ins[0].wait()
    ins[1].wait()
    pl.semaphore_wait(barrier, 2 * (GROUP - 1) + NREP - 1)

    def spread(half, d, dx):
        r = rank(mod(RING - d, RING))
        put(table.at[base[half]], table.at[base[half] + 2 * r + dx],
            first_send.at[half], first_recv.at[half, r], peer(half, d, dx))

    for half in range(2):
        spread(half, jnp.int32(0), 1)

    @pl.loop(0, RING - 1)
    def _(k):
        for half in range(2):
            spread(half, far_first(k), 1)

    @pl.loop(0, RING - 1)
    def _(k):
        for half in range(2):
            spread(half, far_first(k), 0)

    ins[2].wait()

    @pl.loop(1, NREP)
    def _(p):
        put(cot_all.at[rep], cot_all.at[rep], cot_send, cot_recv, row, mod(rep + p, NREP))

    mine = (z, y)
    ahead = [
        [[peer(1 - half, RING + sign * d) for d in (1, 2)] for sign in (1, -1)]
        for half in range(2)
    ]
    from_two = [[mod(mine[half] + RING - 2 * sign, RING) for sign in (1, -1)] for half in range(2)]

    def piece(half, grp, q, n=PER):
        return table.at[pl.ds(half * RING * GROUP + grp * GROUP + q * PER, n)]

    def own_piece(q, n=PER):
        for half in range(2):
            waits(piece(half, mine[half], q, n), first_recv.at[half, q])
            ref = piece(half, mine[half], q)
            for side in range(2):
                put(ref, ref, ring_send.at[half, side], two_recv.at[half, side, q],
                    ahead[half][side][1])

    def pass_piece(q):
        for half in range(2):
            for side in range(2):
                ref = piece(half, from_two[half][side], q)
                waits(ref, two_recv.at[half, side, q])
                put(ref, ref, ring_send.at[half, side], rest_recv.at[half, side, 1],
                    ahead[half][side][0])

                @pl.when(mod(q, 2) == side)
                def _():
                    put(ref, ref, ring_send.at[half, side], rest_recv.at[half, side, 2],
                        ahead[half][side][1])

    own_piece(0, 1)

    @pl.loop(1, LEAD)
    def _(q):
        own_piece(q)

    @pl.loop(LEAD, SUB)
    def _(q):
        own_piece(q)
        pass_piece(q - LEAD)

    @pl.loop(SUB - LEAD, SUB)
    def _(q):
        pass_piece(q)

    for half in range(2):
        for side in range(2):
            ref = piece(half, mine[half], 0, GROUP)
            put(ref, ref, ring_send.at[half, side], rest_recv.at[half, side, 0],
                ahead[half][side][0])

    for c in ins[3:]:
        c.wait()
    w_t[...] = weight[...].astype(jnp.float32).T.astype(jnp.bfloat16)
    count = count_ref[0]

    @pl.loop(0, SLOTS)
    def _(s):
        col = cols_ref[s]
        blk = lax.div(col, jnp.int32(2))
        by = lax.div(blk, jnp.int32(NX * NZ))
        dx = mod(lax.div(blk, jnp.int32(NZ)) + xh, NX)
        bz = mod(blk, NZ)
        place_a = bz * GROUP + rank(mod(by - y + NY, NY)) * 2 + dx
        place_b = RING * GROUP + by * GROUP + rank(mod(bz - z + NZ, NZ)) * 2 + dx
        index_s[s] = jnp.where(mod(col, 2) == 0, place_a, place_b)
        code_s[s] = jnp.where(s < count, rows_ref[s], 2)

    for kind in range(3):
        for half in range(2):
            for side in range(2):
                waits(table.at[pl.ds(0, (GROUP, GROUP, GROUP // 2)[kind])],
                      rest_recv.at[half, side, kind])

    load.wait()

    def batch(b, acc):
        picks = []
        for j in range(BATCH):
            s = b * BATCH + j
            tile = table[index_s[s]]
            r = code_s[s]
            zero = jnp.zeros_like(tile)
            up = jnp.where(r == 0, tile, zero)
            down = jnp.where(r == 1, tile, zero)
            picks.append(jnp.concatenate([up, down], axis=0))
        lhs = jnp.concatenate(picks, axis=1)
        rhs = jnp.concatenate([tv[b * BATCH + j] for j in range(BATCH)], axis=1)
        return acc + lax.dot_general(
            lhs, rhs, (((1,), (1,)), ((), ())), preferred_element_type=jnp.float32
        )

    acc = lax.fori_loop(0, SLOTS // BATCH, batch, jnp.zeros((64, TILE), jnp.float32))
    agg = jnp.concatenate([acc[:32], acc[32:]], axis=1).astype(jnp.bfloat16)
    agg_all[rep] = agg

    @pl.loop(1, NREP)
    def _(p):
        put(agg_all.at[rep], agg_all.at[rep], agg_send, agg_recv, row, mod(rep + p, NREP))

    three = pl.ds(0, NREP - 1)
    waits(cot_all.at[three], cot_recv)
    waits(agg_all.at[three], agg_recv)

    full = agg_all[...].reshape(4 * 32, 2 * TILE)
    pre_t = jnp.dot(w_t[...], full, preferred_element_type=jnp.float32)
    gate = jax.nn.sigmoid(pre_t)
    slope = gate + pre_t * gate * (1.0 - gate)
    cot = cot_all[...].reshape(4 * 64, 2 * TILE).astype(jnp.float32)
    d_pre_t = (cot * slope).astype(jnp.bfloat16)
    grad = lax.dot_general(
        agg, d_pre_t, (((1,), (1,)), ((), ())), preferred_element_type=jnp.float32
    )
    for j in range(8):
        rs_src[j] = grad[8 * (j // 2):8 * (j // 2) + 8, TILE * (j % 2):TILE * (j % 2) + TILE]

    @pl.loop(0, NY - 1)
    def _(k):
        other = mod(y + far_first(k), NY)
        put(rs_src.at[other], rs_buf.at[y], rs_send, rs_recv, at(other, xh, z))

    rs_buf[y] = rs_src[y]

    own_t = jnp.dot(
        w_t[pl.ds(pl.multiple_of(rep * 64, 64), 64), :], full, preferred_element_type=jnp.float32
    )
    hidden_ref[...] = (own_t * jax.nn.sigmoid(own_t)).astype(jnp.bfloat16)

    seven = pl.ds(0, RING - 1)
    waits(rs_buf.at[seven], rs_recv)
    total = rs_buf[0]
    for j in range(1, NY):
        total = total + rs_buf[j]
    mid_src[...] = total
    g_z = z * NX + xh

    @pl.loop(0, RING - 1)
    def _(k):
        z_to = mod(z + far_first(k), NZ)
        put(mid_src, mid_buf.at[g_z], mid_send, mid_recv, at(y, 1 - xh, z_to))
        put(mid_src, mid_buf.at[g_z], mid_send, mid_recv, at(y, xh, z_to))

    put(mid_src, mid_buf.at[g_z], mid_send, mid_recv, at(y, 1 - xh, z))
    mid_buf[g_z] = total

    fifteen = pl.ds(0, GROUP - 1)
    waits(mid_buf.at[fifteen], mid_recv)
    total = mid_buf[0]
    for j in range(1, GROUP):
        total = total + mid_buf[j]
    end_buf[y] = total

    @pl.loop(0, RING - 1)
    def _(k):
        put(end_buf.at[y], end_buf.at[y], end_send, end_recv, peer(0, far_first(k)))

    for half in range(2):
        waits(table.at[pl.ds(0, GROUP - 1)], first_send.at[half])
        for side in range(2):
            waits(table.at[pl.ds(0, 7 * GROUP // 2)], ring_send.at[half, side])
    waits(cot_all.at[three], cot_send)
    waits(agg_all.at[three], agg_send)
    waits(rs_buf.at[seven], rs_send)
    waits(mid_buf.at[fifteen], mid_send)

    waits(end_buf.at[seven], end_recv)
    for j in range(8):
        dw_ref[8 * (j // 2):8 * (j // 2) + 8, TILE * (j % 2):TILE * (j % 2) + TILE] = end_buf[j]

    waits(end_buf.at[seven], end_send)


def shards(features_t, tile_values, tile_rows, tile_cols, tile_count, weight, cotangent):
    vmem = pl.BlockSpec(memory_space=pltpu.VMEM)
    hbm = pl.BlockSpec(memory_space=pl.ANY)
    dma = pltpu.SemaphoreType.DMA
    bf16, f32 = jnp.bfloat16, jnp.float32
    hidden_t, d_weight = pl.pallas_call(
        kernel,
        out_shape=(
            pltpu.VMEM((64, 256), bf16),
            pltpu.VMEM((32, 256), f32),
        ),
        in_specs=[hbm] * 7,
        out_specs=(vmem, vmem),
        scratch_shapes=[
            pltpu.SMEM((SLOTS,), jnp.int32),
            pltpu.SMEM((SLOTS,), jnp.int32),
            pltpu.SMEM((1,), jnp.int32),
            pltpu.SMEM((SLOTS,), jnp.int32),
            pltpu.SMEM((SLOTS,), jnp.int32),
            pltpu.VMEM((2 * RING * GROUP, 32, TILE), bf16),
            pltpu.VMEM((SLOTS, TILE, TILE), bf16),
            pltpu.VMEM((128, 256), bf16),
            pltpu.VMEM((NREP, 64, 256), bf16),
            pltpu.VMEM((NREP, 32, 256), bf16),
            pltpu.VMEM((256, 128), bf16),
            pltpu.VMEM((8, 8, TILE), f32),
            pltpu.VMEM((8, 8, TILE), f32),
            pltpu.VMEM((8, TILE), f32),
            pltpu.VMEM((GROUP, 8, TILE), f32),
            pltpu.VMEM((8, 8, TILE), f32),
            dma(()), dma((7,)), dma((2,)), dma((2, SUB)),
            dma((2, 2)), dma((2, 2, SUB)), dma((2, 2, 3)),
            dma(()), dma(()), dma(()), dma(()),
            dma(()), dma(()), dma(()), dma(()), dma(()), dma(()),
        ],
        compiler_params=pltpu.CompilerParams(
            collective_id=0, has_side_effects=True, vmem_limit_bytes=56 * 1024 * 1024
        ),
        name="layer",
    )(tile_rows, tile_cols, tile_count, features_t, tile_values, weight, cotangent.T)
    return hidden_t.T, d_weight


def solution(mesh):
    placed = (
        P("rep", "row"),
        P("row", None, None),
        P("row"),
        P("row"),
        P("row"),
        P(),
        P("row", "rep"),
    )
    return jax.shard_map(
        shards,
        mesh=mesh,
        in_specs=placed,
        out_specs=(P("row", "rep"), P("rep", None)),
        check_vma=False,
    )
```

```python
import jax
import jax.numpy as jnp
from jax import lax
from jax.experimental import pallas as pl
from jax.experimental.pallas import tpu as pltpu
from jax.sharding import PartitionSpec as P

MESH = pl.DeviceIdType.MESH
NY, NX, NZ, NREP = 8, 2, 8, 4
RING = 8
GROUP = 16
SUB = 8
LEAD = 7
PER = GROUP // SUB
TILE = 128
SLOTS = 128
BATCH = 32


def mod(a, n):
    return lax.rem(a, jnp.int32(n))


def rank(d):
    return jnp.where(d == 0, 0, jnp.where(d <= RING // 2, 2 * d - 1, 2 * (RING - d)))


def far_first(k):
    return RING // 2 + lax.div(k + 1, jnp.int32(2)) * (1 - 2 * mod(k, 2))


def near_first(k):
    near = lax.div(k, jnp.int32(2)) + 1
    return jnp.where(mod(k, 2) == 0, near, RING - near)


def kernel(
    rows_hbm, cols_hbm, count_hbm, feat_hbm, tv_hbm, weight_hbm, cot_hbm,
    hidden_ref, dw_ref,
    rows_ref, cols_ref, count_ref, index_s, code_s,
    table, tv, weight, cot_all, agg_all, w_t, rs_src, rs_buf, mid_src, mid_buf, end_buf,
    tv_sem, in_sem, first_send, first_recv, ring_send, two_recv, rest_recv,
    cot_send, cot_recv, agg_send, agg_recv,
    rs_send, rs_recv, mid_send, mid_recv, end_send, end_recv,
):
    row = lax.axis_index("row")
    rep = lax.axis_index("rep")
    y = lax.div(row, jnp.int32(NX * NZ))
    xh = mod(lax.div(row, jnp.int32(NZ)), NX)
    z = mod(row, NZ)

    def at(y_, x_, z_):
        return (y_ * NX + x_) * NZ + z_

    def peer(half, d, dx=0):
        x_ = mod(xh + dx, NX)
        return at(mod(y + d, NY), x_, z) if half == 0 else at(y, x_, mod(z + d, NZ))

    def waits(ref, sem):
        pltpu.make_async_copy(ref, ref, sem).wait()

    def put(src, dst, send_sem, recv_sem, to, rep_to=None):
        pltpu.make_async_remote_copy(
            src_ref=src, dst_ref=dst, send_sem=send_sem, recv_sem=recv_sem,
            device_id=(to, rep if rep_to is None else rep_to), device_id_type=MESH,
        ).start()

    barrier = pltpu.get_barrier_semaphore()

    def greet(to, rep_to):
        pl.semaphore_signal(barrier, inc=1, device_id=(to, rep_to), device_id_type=MESH)

    @pl.loop(0, RING - 1)
    def _(k):
        d = far_first(k)
        for half in range(2):
            greet(peer(half, d, 1), rep)
            greet(peer(half, d), rep)

    for half in range(2):
        greet(peer(half, 0, 1), rep)

    @pl.loop(1, NREP)
    def _(p):
        greet(row, mod(rep + p, NREP))

    base = (z * GROUP, RING * GROUP + y * GROUP)
    ins = [
        pltpu.make_async_copy(feat_hbm.at[:, pl.ds(0, TILE)], table.at[base[0]], in_sem.at[0]),
        pltpu.make_async_copy(feat_hbm.at[:, pl.ds(TILE, TILE)], table.at[base[1]], in_sem.at[1]),
        pltpu.make_async_copy(cot_hbm, cot_all.at[rep], in_sem.at[2]),
        pltpu.make_async_copy(weight_hbm, weight, in_sem.at[3]),
        pltpu.make_async_copy(rows_hbm, rows_ref, in_sem.at[4]),
        pltpu.make_async_copy(cols_hbm, cols_ref, in_sem.at[5]),
        pltpu.make_async_copy(count_hbm, count_ref, in_sem.at[6]),
    ]
    for c in ins:
        c.start()
    load = pltpu.make_async_copy(tv_hbm, tv, tv_sem)
    load.start()
    ins[0].wait()
    ins[1].wait()
    pl.semaphore_wait(barrier, 2 * (GROUP - 1) + NREP - 1)

    def spread(half, d, dx):
        r = rank(mod(RING - d, RING))
        put(table.at[base[half]], table.at[base[half] + 2 * r + dx],
            first_send.at[half], first_recv.at[half, r], peer(half, d, dx))

    for half in range(2):
        spread(half, jnp.int32(0), 1)

    @pl.loop(0, RING - 1)
    def _(k):
        for half in range(2):
            spread(half, far_first(k), 1)

    @pl.loop(0, RING - 1)
    def _(k):
        for half in range(2):
            spread(half, near_first(k), 0)

    ins[2].wait()

    @pl.loop(1, NREP)
    def _(p):
        put(cot_all.at[rep], cot_all.at[rep], cot_send, cot_recv, row, mod(rep + p, NREP))

    mine = (z, y)
    ahead = [
        [[peer(1 - half, RING + sign * d) for d in (1, 2)] for sign in (1, -1)]
        for half in range(2)
    ]
    from_two = [[mod(mine[half] + RING - 2 * sign, RING) for sign in (1, -1)] for half in range(2)]

    def piece(half, grp, q, n=PER):
        return table.at[pl.ds(half * RING * GROUP + grp * GROUP + q * PER, n)]

    def own_piece(q, n=PER):
        for half in range(2):
            waits(piece(half, mine[half], q, n), first_recv.at[half, q])
            ref = piece(half, mine[half], q)
            for side in range(2):
                put(ref, ref, ring_send.at[half, side], two_recv.at[half, side, q],
                    ahead[half][side][1])

    def pass_piece(q):
        for half in range(2):
            for side in range(2):
                ref = piece(half, from_two[half][side], q)
                waits(ref, two_recv.at[half, side, q])
                put(ref, ref, ring_send.at[half, side], rest_recv.at[half, side, 1],
                    ahead[half][side][0])

                @pl.when(mod(q, 2) == side)
                def _():
                    put(ref, ref, ring_send.at[half, side], rest_recv.at[half, side, 2],
                        ahead[half][side][1])

    own_piece(0, 1)

    @pl.loop(1, LEAD)
    def _(q):
        own_piece(q)

    @pl.loop(LEAD, SUB)
    def _(q):
        own_piece(q)
        pass_piece(q - LEAD)

    @pl.loop(SUB - LEAD, SUB)
    def _(q):
        pass_piece(q)

    for half in range(2):
        for side in range(2):
            ref = piece(half, mine[half], 0, GROUP)
            put(ref, ref, ring_send.at[half, side], rest_recv.at[half, side, 0],
                ahead[half][side][0])

    for c in ins[3:]:
        c.wait()
    w_t[...] = weight[...].astype(jnp.float32).T.astype(jnp.bfloat16)
    count = count_ref[0]

    @pl.loop(0, SLOTS)
    def _(s):
        col = cols_ref[s]
        blk = lax.div(col, jnp.int32(2))
        by = lax.div(blk, jnp.int32(NX * NZ))
        dx = mod(lax.div(blk, jnp.int32(NZ)) + xh, NX)
        bz = mod(blk, NZ)
        place_a = bz * GROUP + rank(mod(by - y + NY, NY)) * 2 + dx
        place_b = RING * GROUP + by * GROUP + rank(mod(bz - z + NZ, NZ)) * 2 + dx
        index_s[s] = jnp.where(mod(col, 2) == 0, place_a, place_b)
        code_s[s] = jnp.where(s < count, rows_ref[s], 2)

    for kind in range(3):
        for half in range(2):
            for side in range(2):
                waits(table.at[pl.ds(0, (GROUP, GROUP, GROUP // 2)[kind])],
                      rest_recv.at[half, side, kind])

    load.wait()

    def batch(b, acc):
        picks = []
        for j in range(BATCH):
            s = b * BATCH + j
            tile = table[index_s[s]]
            r = code_s[s]
            zero = jnp.zeros_like(tile)
            up = jnp.where(r == 0, tile, zero)
            down = jnp.where(r == 1, tile, zero)
            picks.append(jnp.concatenate([up, down], axis=0))
        lhs = jnp.concatenate(picks, axis=1)
        rhs = jnp.concatenate([tv[b * BATCH + j] for j in range(BATCH)], axis=1)
        return acc + lax.dot_general(
            rhs, lhs, (((1,), (1,)), ((), ())), preferred_element_type=jnp.float32
        )

    acc = lax.fori_loop(0, SLOTS // BATCH, batch, jnp.zeros((TILE, 64), jnp.float32)).T
    agg = jnp.concatenate([acc[:32], acc[32:]], axis=1).astype(jnp.bfloat16)
    agg_all[rep] = agg

    @pl.loop(1, NREP)
    def _(p):
        put(agg_all.at[rep], agg_all.at[rep], agg_send, agg_recv, row, mod(rep + p, NREP))

    three = pl.ds(0, NREP - 1)
    waits(cot_all.at[three], cot_recv)
    waits(agg_all.at[three], agg_recv)

    full = agg_all[...].reshape(4 * 32, 2 * TILE)
    pre_t = jnp.dot(w_t[...], full, preferred_element_type=jnp.float32)
    gate = jax.nn.sigmoid(pre_t)
    slope = gate + pre_t * gate * (1.0 - gate)
    cot = cot_all[...].reshape(4 * 64, 2 * TILE).astype(jnp.float32)
    d_pre_t = (cot * slope).astype(jnp.bfloat16)
    grad = lax.dot_general(
        agg, d_pre_t, (((1,), (1,)), ((), ())), preferred_element_type=jnp.float32
    )
    for j in range(8):
        rs_src[j] = grad[8 * (j // 2):8 * (j // 2) + 8, TILE * (j % 2):TILE * (j % 2) + TILE]

    @pl.loop(0, NY - 1)
    def _(k):
        other = mod(y + far_first(k), NY)
        put(rs_src.at[other], rs_buf.at[y], rs_send, rs_recv, at(other, xh, z))

    rs_buf[y] = rs_src[y]

    own_t = jnp.dot(
        w_t[pl.ds(pl.multiple_of(rep * 64, 64), 64), :], full, preferred_element_type=jnp.float32
    )
    hidden_ref[...] = (own_t * jax.nn.sigmoid(own_t)).astype(jnp.bfloat16)

    seven = pl.ds(0, RING - 1)
    waits(rs_buf.at[seven], rs_recv)
    total = rs_buf[0]
    for j in range(1, NY):
        total = total + rs_buf[j]
    mid_src[...] = total
    g_z = z * NX + xh

    @pl.loop(0, RING - 1)
    def _(k):
        z_to = mod(z + far_first(k), NZ)
        put(mid_src, mid_buf.at[g_z], mid_send, mid_recv, at(y, 1 - xh, z_to))
        put(mid_src, mid_buf.at[g_z], mid_send, mid_recv, at(y, xh, z_to))

    put(mid_src, mid_buf.at[g_z], mid_send, mid_recv, at(y, 1 - xh, z))
    mid_buf[g_z] = total

    fifteen = pl.ds(0, GROUP - 1)
    waits(mid_buf.at[fifteen], mid_recv)
    total = mid_buf[0]
    for j in range(1, GROUP):
        total = total + mid_buf[j]
    end_buf[y] = total

    @pl.loop(0, RING - 1)
    def _(k):
        put(end_buf.at[y], end_buf.at[y], end_send, end_recv, peer(0, far_first(k)))

    for half in range(2):
        waits(table.at[pl.ds(0, GROUP - 1)], first_send.at[half])
        for side in range(2):
            waits(table.at[pl.ds(0, 7 * GROUP // 2)], ring_send.at[half, side])
    waits(cot_all.at[three], cot_send)
    waits(agg_all.at[three], agg_send)
    waits(rs_buf.at[seven], rs_send)
    waits(mid_buf.at[fifteen], mid_send)

    waits(end_buf.at[seven], end_recv)
    for j in range(8):
        dw_ref[8 * (j // 2):8 * (j // 2) + 8, TILE * (j % 2):TILE * (j % 2) + TILE] = end_buf[j]

    waits(end_buf.at[seven], end_send)


def shards(features_t, tile_values, tile_rows, tile_cols, tile_count, weight, cotangent):
    vmem = pl.BlockSpec(memory_space=pltpu.VMEM)
    hbm = pl.BlockSpec(memory_space=pl.ANY)
    dma = pltpu.SemaphoreType.DMA
    bf16, f32 = jnp.bfloat16, jnp.float32
    hidden_t, d_weight = pl.pallas_call(
        kernel,
        out_shape=(
            pltpu.VMEM((64, 256), bf16),
            pltpu.VMEM((32, 256), f32),
        ),
        in_specs=[hbm] * 7,
        out_specs=(vmem, vmem),
        scratch_shapes=[
            pltpu.SMEM((SLOTS,), jnp.int32),
            pltpu.SMEM((SLOTS,), jnp.int32),
            pltpu.SMEM((1,), jnp.int32),
            pltpu.SMEM((SLOTS,), jnp.int32),
            pltpu.SMEM((SLOTS,), jnp.int32),
            pltpu.VMEM((2 * RING * GROUP, 32, TILE), bf16),
            pltpu.VMEM((SLOTS, TILE, TILE), bf16),
            pltpu.VMEM((128, 256), bf16),
            pltpu.VMEM((NREP, 64, 256), bf16),
            pltpu.VMEM((NREP, 32, 256), bf16),
            pltpu.VMEM((256, 128), bf16),
            pltpu.VMEM((8, 8, TILE), f32),
            pltpu.VMEM((8, 8, TILE), f32),
            pltpu.VMEM((8, TILE), f32),
            pltpu.VMEM((GROUP, 8, TILE), f32),
            pltpu.VMEM((8, 8, TILE), f32),
            dma(()), dma((7,)), dma((2,)), dma((2, SUB)),
            dma((2, 2)), dma((2, 2, SUB)), dma((2, 2, 3)),
            dma(()), dma(()), dma(()), dma(()),
            dma(()), dma(()), dma(()), dma(()), dma(()), dma(()),
        ],
        compiler_params=pltpu.CompilerParams(
            collective_id=0, has_side_effects=True, vmem_limit_bytes=56 * 1024 * 1024
        ),
        name="layer",
    )(tile_rows, tile_cols, tile_count, features_t, tile_values, weight, cotangent.T)
    return hidden_t.T, d_weight


def solution(mesh):
    placed = (
        P("rep", "row"),
        P("row", None, None),
        P("row"),
        P("row"),
        P("row"),
        P(),
        P("row", "rep"),
    )
    return jax.shard_map(
        shards,
        mesh=mesh,
        in_specs=placed,
        out_specs=(P("row", "rep"), P("rep", None)),
        check_vma=False,
    )
```
